32 devices in a mesh: st: 8 (over z, x), ch: 4 (over y, core).
Axes of the slice: x: 2, y: 2, z: 4, core: 2. Of those that a mesh axis runs over, the one named last changes fastest.
Arguments:
- waveform: bfloat16 [256, 3, 8704], P('st'), may hold values from -500 to 500
- templates: bfloat16 [416, 32, 512], P('st', 'ch'), may hold values from -50 to 50
- block_of: int32 [4, 416, 2], P('ch'), may hold values from 0 to 7, all different within a row; in each aligned block of 52 rows (0 to 51, 52 to 103, ..., all dimensions but the last counted through in order) at most 17 rows name the same one
- trace_of: int32 [4, 8, 8, 4], P('ch'), may hold values from 0 to 95
Outputs:
- detection: float32 [416, 8192], P('st', 'ch')
The draws below stay inside these ranges and needn't reach their ends.
Inputs may be any that keep to these rules, and one draw needn't show every extreme that they name: `block_of`: a row names two different station blocks; among the 52 templates of one owner (aligned blocks of the template dimension) in one group, no station block is named by more than 17 templates, and some station block is named by exactly 17.
All inputs are finite; a program needn't handle non-finite values.
Results may differ from the reference program's by a relative error of at most 0.00035.
Values may be sent and summed in bfloat16 or wider, within the bound.
A program may use at most 192 MiB of HBM per device.

```python
import math
import jax
import jax.numpy as jnp
import numpy as np
from jax import lax

CHANS = 32
TAPS = 512
K_DEV = 52
S_DEV = 32
CH_DEV = 8
HALF = 4
GROUPS = 4
BLOCKS = 8
OWNERS = 8
TEMPLATES = 416
STATIONS = 256
LAGS = 8192
WIN = 8704
SLOTS = 17


def draw_waveform(key, part):
    key_base, key_trace, key_block = jax.random.split(jax.random.fold_in(key, 11), 3)
    full_shape = (STATIONS, 3, WIN)
    pieces = (WIN + 31) // 32
    noise_base = jax.random.truncated_normal(key_base, -5.0, 5.0, full_shape, jnp.float32)
    log_range = jnp.log(10.0)
    trace_scale = jnp.exp(jax.random.uniform(key_trace, (STATIONS, 3, 1), jnp.float32, 0.0, 1.0) * log_range)
    block_scale = jnp.exp(jax.random.uniform(key_block, (STATIONS, 3, pieces), jnp.float32, 0.0, 1.0) * log_range)
    envelope = jnp.repeat(block_scale, 32, axis=2)[:, :, :WIN]
    return (noise_base * trace_scale * envelope).astype(jnp.bfloat16)


def draw_templates(key, part):
    key_base, key_scale = jax.random.split(jax.random.fold_in(key, 23), 2)
    full_shape = (TEMPLATES, CHANS, TAPS)
    noise_base = jax.random.truncated_normal(key_base, -5.0, 5.0, full_shape, jnp.float32)
    log_range = jnp.log(10.0)
    channel_scale = jnp.exp(jax.random.uniform(key_scale, (TEMPLATES, CHANS, 1), jnp.float32, 0.0, 1.0) * log_range)
    return (noise_base * channel_scale).astype(jnp.bfloat16)


def touch_ends(drawn, rng, least, largest):
    longest = drawn.shape.index(max(drawn.shape))
    spots = []
    for shift in (0, 1):
        where = [jax.random.randint(jax.random.fold_in(rng, axis), (), 0, length) for axis, length in enumerate(drawn.shape)]
        where[longest] = (where[longest] + shift) % drawn.shape[longest]
        spots.append(tuple(where))
    return drawn.at[spots[0]].set(least).at[spots[1]].set(largest)


def deal_out(stream_key, own, number, rows, amount, top, limit, skew):
    order = jax.random.permutation(stream_key, amount)
    packed, usual = shares(amount, rows * top, limit, skew, True), shares(amount, rows * top, limit, skew, False)
    places = jnp.arange(amount)

    def named(lengths, rotation):
        used = int((lengths > 0).sum())
        fixed = max(1, used // 4)
        passed = fixed + (places - fixed + rotation * (used - fixed)) % max(1, amount - fixed)
        return jnp.zeros((amount,), jnp.int32).at[order[jnp.where(places < fixed, places, passed)]].set(jnp.asarray(lengths, jnp.int32))

    lengths = jnp.where(number % 4 == 0, named(packed, number // 4), named(usual, number - number // 4 - 1))
    mixed = jax.random.permutation(jax.random.fold_in(own, 3), amount)
    donor, taker = mixed[0:amount // 2 * 2:2], mixed[1:amount // 2 * 2:2]
    slack = jnp.minimum(lengths[donor] - 1, limit - lengths[taker]) // 2
    slack = jnp.where((donor == order[0]) | (taker == order[0]) | (lengths[taker] == 0), 0, jnp.maximum(slack, 0))
    passed = jax.random.randint(jax.random.fold_in(own, 4), (amount // 2,), 0, 1 << 20) % (slack + 1)
    lengths = lengths.at[donor].add(-passed).at[taker].add(passed)
    items = jnp.searchsorted(jnp.cumsum(lengths), jnp.arange(rows * top), side="right").astype(jnp.int32)
    grid = items.reshape(top, rows).T
    grid = grid[jax.random.permutation(jax.random.fold_in(own, 1), rows)]
    rotation = jax.random.randint(jax.random.fold_in(own, 2), (rows, 1), 0, top)
    return jnp.take_along_axis(grid, (jnp.arange(top)[None, :] + rotation) % top, axis=1)


def shares(number_of, total, bound, slope, full):
    weights = [(1 << 20) // math.isqrt(grade ** slope) + 1 for grade in range(1, number_of + 1)]
    largest = bound if full else min(bound, max(-(-total // number_of), total * weights[0] // sum(weights)))
    least = 1 if total - largest >= number_of - 1 else 0
    given, rest = [largest] + [least] * (number_of - 1), total - largest - least * (number_of - 1)
    while rest > 0:
        free = [i for i in range(1, number_of) if given[i] < largest] or [i for i in range(1, number_of) if given[i] < bound]
        pool, budget = sum([weights[i] for i in free]), rest
        for i in free:
            more = min(bound - given[i], max(1, budget * weights[i] // pool), rest)
            given[i] = given[i] + more
            rest = rest - more
    return np.array(given)


def setup_inputs(seed: int = 0) -> dict:
    arg_keys = jax.random.split(jax.random.key(seed), 5)
    waveform = draw_waveform(jax.random.fold_in(arg_keys[4], 71), 0)
    templates = draw_templates(jax.random.fold_in(arg_keys[4], 71), 0)
    block_of_keys = jax.random.split(jax.random.fold_in(arg_keys[2], 1), GROUPS * TEMPLATES // K_DEV)
    block_of_turns = jax.random.permutation(jax.random.fold_in(arg_keys[2], 3), GROUPS * TEMPLATES // K_DEV)
    block_of = jax.vmap(lambda own, number: deal_out(jax.random.fold_in(arg_keys[2], 2), own, number, K_DEV, BLOCKS, 2, SLOTS, 2))(block_of_keys, block_of_turns).reshape((GROUPS, TEMPLATES, 2))
    trace_of = touch_ends(jax.random.randint(arg_keys[3], (GROUPS, OWNERS, BLOCKS, HALF), 0, 3 * S_DEV), jax.random.fold_in(arg_keys[3], 1), 0, (3 * S_DEV) - 1).astype(jnp.int32)
    return {"waveform": waveform, "templates": templates, "block_of": block_of, "trace_of": trace_of}


EPSILON = 1e-05

def reference(waveform, templates, block_of, trace_of):
    rows_all = waveform.reshape(STATIONS * 3, WIN)
    halves = (jnp.arange(CH_DEV) // HALF).astype(jnp.int32)
    chosen_blocks = jnp.take(block_of, halves, axis=2).astype(jnp.int32)
    group_ids = jnp.arange(GROUPS, dtype=jnp.int32)[:, None, None]
    owner_ids = (jnp.arange(TEMPLATES, dtype=jnp.int32) // K_DEV)[None, :, None]
    chan_pos = (jnp.arange(CH_DEV, dtype=jnp.int32) % HALF)[None, None, :]
    picks = trace_of[group_ids, owner_ids, chosen_blocks, chan_pos]
    row_index = (chosen_blocks * (3 * S_DEV) + picks).astype(jnp.int32)
    row_index = jnp.transpose(row_index, (1, 0, 2)).reshape(TEMPLATES, CHANS)
    fft_len = 2 ** (WIN + TAPS).bit_length()
    group_size = math.gcd(TEMPLATES, 32)

    def group_terms(operands):
        index_block, filter_block = operands
        traces = jnp.take(rows_all, index_block, axis=0).astype(jnp.float32)
        filters = filter_block.astype(jnp.float32)
        spectrum = jnp.fft.rfft(traces, fft_len, axis=-1) * jnp.conj(jnp.fft.rfft(filters, fft_len, axis=-1))
        raw_sum = jnp.fft.irfft(spectrum, fft_len, axis=-1)[..., :LAGS]
        energy = lax.reduce_window(traces * traces, jnp.array(0, traces.dtype), lax.add, (1, 1, TAPS), (1, 1, 1), 'VALID')[..., :LAGS]
        filter_power = lax.optimization_barrier(jnp.mean(filters * filters, axis=-1, keepdims=True))
        coherence = raw_sum / (TAPS * jnp.sqrt((energy / TAPS + EPSILON) * (filter_power + EPSILON)))
        return lax.optimization_barrier(jnp.sum(coherence, axis=1))
    result = lax.map(group_terms, (row_index.reshape(-1, group_size, CHANS), templates.reshape(-1, group_size, CHANS, TAPS)))
    return result.reshape(TEMPLATES, LAGS)
```

```python
import functools

import jax
import jax.numpy as jnp
from jax import lax
from jax.experimental import pallas as pl
from jax.experimental.pallas import tpu as pltpu
from jax.sharding import PartitionSpec as P

EPSILON = 1e-05
SHIFTS = 32
GROUP = 4


def correlate_kernel(
    dims, start_ref, order_ref, gain_ref, lanes_ref, filters_ref, out_ref, hankel, skewed, scale
):
    templates, pairs, half, taps, cols, depth = dims
    block = pl.program_id(0)
    width = lanes_ref.shape[-1]

    @pl.when(block == 0)
    def _():
        out_ref[...] = jnp.zeros_like(out_ref)
        hankel[...] = jnp.zeros_like(hankel)

    row = lax.broadcasted_iota(jnp.int32, (SHIFTS, width), 0)
    blocks_per_tap = taps // SHIFTS

    def ahead(x, by):
        return pltpu.roll(x, (x.shape[1] - by) % x.shape[1], 1)

    for c in range(half):
        lanes = lanes_ref[0, c].astype(jnp.float32)
        for q in range(blocks_per_tap + 1):
            moved = lanes if q == 0 else ahead(lanes, q)
            hankel[c, q * SHIFTS : (q + 1) * SHIFTS, :] = moved[:, :cols].astype(jnp.bfloat16)
        squares = lanes * lanes
        prefix, suffix = squares, squares
        step = 1
        while step < SHIFTS:
            prefix = prefix + jnp.where(row >= step, pltpu.roll(prefix, step, 0), 0.0)
            suffix = suffix + jnp.where(
                row < SHIFTS - step, pltpu.roll(suffix, SHIFTS - step, 0), 0.0
            )
            step *= 2
        before = jnp.where(row >= 1, pltpu.roll(prefix, 1, 0), 0.0)
        total = jnp.broadcast_to(jnp.sum(squares, axis=0, keepdims=True), (SHIFTS, width))
        middle, at, power, run = jnp.zeros_like(total), 1, 1, total
        count = blocks_per_tap - 1
        while count:
            if count & 1:
                middle = middle + ahead(run, at)
                at += power
            count >>= 1
            if count:
                run = run + ahead(run, power)
                power *= 2
        energy = suffix + middle + ahead(before, blocks_per_tap)
        scale[c] = lax.rsqrt(energy[:, :cols] / taps + EPSILON)

    first, last = start_ref[block], start_ref[block + 1]

    def chunk(number, carry):
        base = first + number * GROUP
        for g in range(GROUP):
            pair = order_ref[base + g]
            rows = filters_ref[pair]
            for c in range(half):
                spread = jnp.broadcast_to(rows[c : c + 1], (SHIFTS, depth))
                spread = pltpu.roll(spread, 0, 1, stride=1, stride_axis=0)
                skewed[c, g * SHIFTS : (g + 1) * SHIFTS, :] = spread.astype(jnp.bfloat16)
        totals = [None] * GROUP
        for c in range(half):
            raw = jnp.dot(skewed[c], hankel[c], preferred_element_type=jnp.float32)
            for g in range(GROUP):
                pair = order_ref[base + g]
                term = raw[g * SHIFTS : (g + 1) * SHIFTS] * (scale[c] * gain_ref[pair * half + c])
                totals[g] = term if c == 0 else totals[g] + term
        for g in range(GROUP):
            place = jnp.where(base + g < last, lax.div(order_ref[base + g], 2), templates)
            out_ref[place] += totals[g]
        return carry

    lax.fori_loop(0, lax.div(last - first + GROUP - 1, GROUP), chunk, 0)


def correlate(arrived, filters, sources):
    blocks, half, window = arrived.shape
    templates = filters.shape[0]
    taps = filters.shape[2]
    pairs = templates * 2
    lags = window - taps
    cols = lags // SHIFTS
    used = window // SHIFTS
    width = -(-used // 128) * 128
    depth = -(-(taps + SHIFTS) // 128) * 128

    lanes = arrived.reshape(blocks, half, used, SHIFTS).transpose(0, 1, 3, 2)
    lanes = jnp.pad(lanes, ((0, 0), (0, 0), (0, 0), (0, width - used)))
    wide = filters.astype(jnp.float32)
    gain = 1.0 / (taps * jnp.sqrt(jnp.mean(wide * wide, axis=2) + EPSILON))
    padded = jnp.pad(wide.reshape(pairs, half, taps), ((0, 0), (0, 0), (0, depth - taps)))

    named = sources.reshape(pairs)
    ids = jnp.arange(pairs, dtype=jnp.int32)
    ahead = (named[None, :] < named[:, None]) | (
        (named[None, :] == named[:, None]) & (ids[None, :] < ids[:, None])
    )
    place = jnp.sum(ahead.astype(jnp.int32), axis=1)
    spots = jnp.arange(pairs + GROUP, dtype=jnp.int32)
    order = jnp.sum(jnp.where(place[None, :] == spots[:, None], ids[None, :], 0), axis=1)
    edges = jnp.arange(blocks + 1, dtype=jnp.int32)
    start = jnp.sum((named[None, :] < edges[:, None]).astype(jnp.int32), axis=1)

    dims = (templates, pairs, half, taps, cols, depth)
    smem = pl.BlockSpec(memory_space=pltpu.SMEM)
    return pl.pallas_call(
        functools.partial(correlate_kernel, dims),
        grid=(blocks,),
        out_shape=jax.ShapeDtypeStruct((templates + 1, SHIFTS, cols), jnp.float32),
        in_specs=[
            smem,
            smem,
            smem,
            pl.BlockSpec((1, half, SHIFTS, width), lambda b: (b, 0, 0, 0)),
            pl.BlockSpec((pairs, half, depth), lambda b: (0, 0, 0)),
        ],
        out_specs=pl.BlockSpec((templates + 1, SHIFTS, cols), lambda b: (0, 0, 0)),
        scratch_shapes=[
            pltpu.VMEM((half, depth, cols), jnp.bfloat16),
            pltpu.VMEM((half, GROUP * SHIFTS, depth), jnp.bfloat16),
            pltpu.VMEM((half, SHIFTS, cols), jnp.float32),
        ],
        compiler_params=pltpu.CompilerParams(vmem_limit_bytes=40 * 1024 * 1024),
        name="correlate",
    )(start, order, gain.reshape(-1), lanes, padded)


def per_device(waveform, templates, block_of, trace_of):
    own_index = lax.axis_index("st")
    station_count = lax.axis_size("st")
    own_templates = templates.shape[0]
    group_chans = templates.shape[1]
    half_chans = group_chans // 2
    window = waveform.shape[2]
    local_rows = waveform.reshape(-1, window)
    sources = block_of[0].reshape(station_count, own_templates, 2)
    own_sources = lax.dynamic_index_in_dim(sources, own_index, 0, keepdims=False)
    wanted = lax.dynamic_index_in_dim(trace_of[0], own_index, 1, keepdims=False)
    source_rows = jnp.take(local_rows, wanted.reshape(-1), axis=0)
    arrived = lax.all_to_all(
        source_rows.reshape(station_count, half_chans, window),
        "st",
        split_axis=0,
        concat_axis=0,
        tiled=True,
    )
    sums = correlate(arrived, templates, own_sources)[:own_templates]
    partial_value = sums.transpose(0, 2, 1).reshape(own_templates, -1)
    return lax.psum_scatter(partial_value, "ch", scatter_dimension=1, tiled=True)


def solution(mesh):
    in_specs = (
        P("st", None, None),
        P("st", "ch", None),
        P("ch", None, None),
        P("ch", None, None, None),
    )
    out_specs = P("st", "ch")
    return jax.shard_map(
        per_device, mesh=mesh, in_specs=in_specs, out_specs=out_specs, check_vma=False
    )
```

```python
import functools

import jax
import jax.numpy as jnp
from jax import lax
from jax.experimental import pallas as pl
from jax.experimental.pallas import tpu as pltpu
from jax.sharding import PartitionSpec as P

EPSILON = 1e-05
SHIFTS = 32
LANES = 128
GROUP = 4


def correlate_kernel(
    dims,
    me_ref,
    start_ref,
    order_ref,
    gain_ref,
    lanes_ref,
    filters_ref,
    keep_ref,
    send_ref,
    totals_ref,
    padded,
    hankel,
    skewed,
    scale,
    turned,
):
    templates, half, taps, used, depth, parts = dims
    block = pl.program_id(0)

    @pl.when(block == 0)
    def _():
        totals_ref[...] = jnp.zeros_like(totals_ref)
        hankel[...] = jnp.zeros_like(hankel)
        padded[...] = jnp.zeros_like(padded)

    row = lax.broadcasted_iota(jnp.int32, (LANES, LANES), 0)
    low = lax.broadcasted_iota(jnp.int32, (SHIFTS, LANES), 1) < LANES // 2
    whole = taps // LANES
    splits = LANES // SHIFTS

    def ahead(x, by):
        by = (LANES - by) % LANES
        return x if by == 0 else pltpu.roll(x, by, 1)

    def strip(x, m):
        at = (m % splits) * SHIFTS
        return x[at : at + SHIFTS]

    def joined(x, m):
        left = ahead(strip(x, m), m // splits)
        right = ahead(strip(x, m + 1), (m + 1) // splits - LANES // 2)
        return jnp.where(low, left, right)

    for c in range(half):
        padded[:used, :] = lanes_ref[0, c].astype(jnp.float32)
        lanes = padded[...].T
        steps = taps // SHIFTS + 1
        for m in range(steps + 2):
            pair = joined(lanes, m).astype(jnp.bfloat16)
            if m < steps:
                hankel[c, m * SHIFTS : (m + 1) * SHIFTS, :LANES] = pair
            if m >= 2:
                hankel[c, (m - 2) * SHIFTS : (m - 1) * SHIFTS, LANES:] = pair
        squares = lanes * lanes
        prefix, suffix = squares, squares
        step = 1
        while step < LANES:
            prefix = prefix + jnp.where(row >= step, pltpu.roll(prefix, step, 0), 0.0)
            suffix = suffix + jnp.where(
                row < LANES - step, pltpu.roll(suffix, LANES - step, 0), 0.0
            )
            step *= 2
        before = jnp.where(row >= 1, pltpu.roll(prefix, 1, 0), 0.0)
        total = jnp.sum(squares, axis=0, keepdims=True)
        middle = jnp.zeros_like(total)
        for by in range(1, whole):
            middle = middle + ahead(total, by)
        energy = suffix + middle + ahead(before, whole)
        root = lax.rsqrt(energy / taps + EPSILON)
        scale[c, :, :LANES] = joined(root, 0)
        scale[c, :, LANES:] = joined(root, 2)

    first, last = start_ref[block], start_ref[block + 1]

    def chunk(number, carry):
        base = first + number * GROUP
        for g in range(GROUP):
            pair = order_ref[base + g]
            rows = filters_ref[pair]
            for c in range(half):
                spread = jnp.broadcast_to(rows[c : c + 1], (SHIFTS, depth))
                spread = pltpu.roll(spread, 0, 1, stride=1, stride_axis=0)
                skewed[c, g * SHIFTS : (g + 1) * SHIFTS, :] = spread.astype(jnp.bfloat16)
        totals = [None] * GROUP
        for c in range(half):
            raw = jnp.dot(skewed[c], hankel[c], preferred_element_type=jnp.float32)
            for g in range(GROUP):
                pair = order_ref[base + g]
                term = raw[g * SHIFTS : (g + 1) * SHIFTS] * (scale[c] * gain_ref[pair * half + c])
                totals[g] = term if c == 0 else totals[g] + term
        for g in range(GROUP):
            place = jnp.where(base + g < last, lax.div(order_ref[base + g], 2), templates)
            totals_ref[place] += totals[g]
        return carry

    lax.fori_loop(0, lax.div(last - first + GROUP - 1, GROUP), chunk, 0)

    @pl.when(block == pl.num_programs(0) - 1)
    def _():
        rows = keep_ref.shape[2]

        def turn(k, carry):
            left, right = totals_ref[k, :, :LANES], totals_ref[k, :, LANES:]
            stack = [left, ahead(left, LANES // 2), right, ahead(right, LANES // 2)]
            lags = jnp.concatenate(stack, axis=0).T
            turned[...] = lags[: LANES // 2]
            for slot in range(parts):
                piece = lax.bitwise_xor(me_ref[0], slot)
                target = send_ref if slot & 1 else keep_ref
                target[slot >> 1, k] = turned[pl.ds(pl.multiple_of(piece * rows, 8), rows), :]
            return carry

        lax.fori_loop(0, templates, turn, 0)


def correlate(arrived, filters, sources, axis):
    blocks, half, window = arrived.shape
    templates = filters.shape[0]
    taps = filters.shape[2]
    pairs = templates * 2
    lags = window - taps
    parts = lax.axis_size(axis)
    cols = lags // SHIFTS
    assert cols == 2 * LANES and LANES == 4 * SHIFTS
    used = window // LANES
    depth = -(-(taps + SHIFTS) // LANES) * LANES
    lanes = arrived.reshape(blocks, half, used, LANES)
    wide = filters.astype(jnp.float32)
    gain = 1.0 / (taps * jnp.sqrt(jnp.mean(wide * wide, axis=2) + EPSILON))
    padded = jnp.pad(wide.reshape(pairs, half, taps), ((0, 0), (0, 0), (0, depth - taps)))

    named = sources.reshape(pairs)
    ids = jnp.arange(pairs, dtype=jnp.int32)
    ahead = (named[None, :] < named[:, None]) | (
        (named[None, :] == named[:, None]) & (ids[None, :] < ids[:, None])
    )
    place = jnp.sum(ahead.astype(jnp.int32), axis=1)
    spots = jnp.arange(pairs + GROUP, dtype=jnp.int32)
    order = jnp.sum(jnp.where(place[None, :] == spots[:, None], ids[None, :], 0), axis=1)
    edges = jnp.arange(blocks + 1, dtype=jnp.int32)
    start = jnp.sum((named[None, :] < edges[:, None]).astype(jnp.int32), axis=1)

    me = lax.axis_index(axis).astype(jnp.int32).reshape(1)
    dims = (templates, half, taps, used, depth, parts)
    smem = pl.BlockSpec(memory_space=pltpu.SMEM)
    piece = (parts // 2, templates, lags // LANES // parts, LANES)
    piece_spec = pl.BlockSpec(piece, lambda b: (0, 0, 0, 0))
    return pl.pallas_call(
        functools.partial(correlate_kernel, dims),
        grid=(blocks,),
        out_shape=[jax.ShapeDtypeStruct(piece, jnp.float32)] * 2,
        in_specs=[
            smem,
            smem,
            smem,
            smem,
            pl.BlockSpec((1, half, used, LANES), lambda b: (b, 0, 0, 0)),
            pl.BlockSpec((pairs, half, depth), lambda b: (0, 0, 0)),
        ],
        out_specs=[piece_spec, piece_spec],
        scratch_shapes=[
            pltpu.VMEM((templates + 1, SHIFTS, cols), jnp.float32),
            pltpu.VMEM((LANES, LANES), jnp.float32),
            pltpu.VMEM((half, depth, cols), jnp.bfloat16),
            pltpu.VMEM((half, GROUP * SHIFTS, depth), jnp.bfloat16),
            pltpu.VMEM((half, SHIFTS, cols), jnp.float32),
            pltpu.VMEM((LANES // 2, LANES), jnp.float32),
        ],
        compiler_params=pltpu.CompilerParams(vmem_limit_bytes=40 * 1024 * 1024),
        name="correlate",
    )(me, start, order, gain.reshape(-1), lanes, padded)


def swapped(x, axis, bit):
    return lax.ppermute(x, axis, [(i, i ^ bit) for i in range(lax.axis_size(axis))])


def per_device(waveform, templates, block_of, trace_of):
    own_index = lax.axis_index("st")
    station_count = lax.axis_size("st")
    own_templates = templates.shape[0]
    group_chans = templates.shape[1]
    half_chans = group_chans // 2
    window = waveform.shape[2]
    sources = block_of[0].reshape(station_count, own_templates, 2)
    own_sources = lax.dynamic_index_in_dim(sources, own_index, 0, keepdims=False)
    wanted = lax.dynamic_index_in_dim(trace_of[0], own_index, 1, keepdims=False)
    source_rows = waveform[wanted.reshape(-1) // 3, wanted.reshape(-1) % 3]
    arrived = lax.all_to_all(
        source_rows.reshape(station_count, half_chans, window),
        "st",
        split_axis=0,
        concat_axis=0,
        tiled=True,
    )
    keep, send = correlate(arrived, templates, own_sources, "ch")
    bit = 1
    while True:
        keep = keep + swapped(send, "ch", bit)
        if keep.shape[0] == 1:
            break
        halves = keep.reshape(keep.shape[0] // 2, 2, *keep.shape[1:])
        keep, send = halves[:, 0], halves[:, 1]
        bit *= 2
    return keep.reshape(own_templates, -1)


def solution(mesh):
    in_specs = (
        P("st", None, None),
        P("st", "ch", None),
        P("ch", None, None),
        P("ch", None, None, None),
    )
    out_specs = P("st", "ch")
    return jax.shard_map(
        per_device, mesh=mesh, in_specs=in_specs, out_specs=out_specs, check_vma=False
    )
```

```python
import functools
import math

import jax
import jax.numpy as jnp
from jax import lax
from jax.experimental import pallas as pl
from jax.experimental.pallas import tpu as pltpu
from jax.sharding import PartitionSpec as P

EPSILON = 1e-05
SHIFTS = 32
LANES = 128
GROUP = 4


def skew_kernel(dims, owner_ref, order_ref, filters_ref, out_ref):
    half, taps, depth, blocks = dims
    chunk = pl.program_id(0)

    @pl.when(owner_ref[chunk] < blocks)
    def _():
        for g in range(GROUP):
            pair = jnp.maximum(order_ref[chunk * GROUP + g], 0)
            rows = filters_ref[lax.shift_right_logical(pair, 1)].astype(jnp.float32)
            rows = jnp.where(lax.bitwise_and(pair, 1) == 1, rows[half:], rows[:half])
            blank = jnp.zeros((SHIFTS, depth - taps), jnp.float32)
            for c in range(half):
                spread = jnp.broadcast_to(rows[c : c + 1], (SHIFTS, taps))
                spread = jnp.concatenate([spread, blank], axis=1)
                spread = pltpu.roll(spread, 0, 1, stride=1, stride_axis=0)
                out_ref[0, c, g * SHIFTS : (g + 1) * SHIFTS, :] = spread.astype(jnp.bfloat16)


def correlate_kernel(
    dims,
    owner_ref,
    order_ref,
    me_ref,
    gain_ref,
    lanes_ref,
    skewed_ref,
    keep_ref,
    send_ref,
    totals_ref,
    padded,
    hankel,
    scale,
    turned,
):
    templates, half, taps, used, parts, blocks = dims
    chunk = pl.program_id(0)
    owner = owner_ref[chunk]
    earlier = owner_ref[jnp.maximum(chunk - 1, 0)]
    fresh = (owner < blocks) & ((chunk == 0) | (owner != earlier))

    @pl.when(chunk == 0)
    def _():
        totals_ref[...] = jnp.zeros_like(totals_ref)
        hankel[...] = jnp.zeros_like(hankel)
        padded[...] = jnp.zeros_like(padded)

    row = lax.broadcasted_iota(jnp.int32, (LANES, LANES), 0)
    low = lax.broadcasted_iota(jnp.int32, (SHIFTS, LANES), 1) < LANES // 2
    whole = taps // LANES
    splits = LANES // SHIFTS

    def ahead(x, by):
        by = (LANES - by) % LANES
        return x if by == 0 else pltpu.roll(x, by, 1)

    def strip(x, m):
        at = (m % splits) * SHIFTS
        return x[at : at + SHIFTS]

    def joined(x, m):
        left = ahead(strip(x, m), m // splits)
        right = ahead(strip(x, m + 1), (m + 1) // splits - LANES // 2)
        return jnp.where(low, left, right)

    @pl.when(fresh)
    def _():
        for c in range(half):
            padded[:used, :] = lanes_ref[0, c].astype(jnp.float32)
            lanes = padded[...].T
            steps = taps // SHIFTS + 1
            for m in range(steps + 2):
                pair = joined(lanes, m).astype(jnp.bfloat16)
                if m < steps:
                    hankel[c, m * SHIFTS : (m + 1) * SHIFTS, :LANES] = pair
                if m >= 2:
                    hankel[c, (m - 2) * SHIFTS : (m - 1) * SHIFTS, LANES:] = pair
            squares = lanes * lanes
            prefix, suffix = squares, squares
            step = 1
            while step < LANES:
                prefix = prefix + jnp.where(row >= step, pltpu.roll(prefix, step, 0), 0.0)
                suffix = suffix + jnp.where(
                    row < LANES - step, pltpu.roll(suffix, LANES - step, 0), 0.0
                )
                step *= 2
            before = jnp.where(row >= 1, pltpu.roll(prefix, 1, 0), 0.0)
            total = jnp.sum(squares, axis=0, keepdims=True)
            middle = jnp.zeros_like(total)
            for by in range(1, whole):
                middle = middle + ahead(total, by)
            energy = suffix + middle + ahead(before, whole)
            root = lax.rsqrt(energy / taps + EPSILON)
            scale[c, :, :LANES] = joined(root, 0)
            scale[c, :, LANES:] = joined(root, 2)

    @pl.when(owner < blocks)
    def _():
        codes = [order_ref[chunk * GROUP + g] for g in range(GROUP)]
        totals = [None] * GROUP
        for c in range(half):
            raw = jnp.dot(skewed_ref[0, c], hankel[c], preferred_element_type=jnp.float32)
            for g in range(GROUP):
                gain = gain_ref[jnp.maximum(codes[g], 0) * half + c]
                term = raw[g * SHIFTS : (g + 1) * SHIFTS] * (scale[c] * gain)
                totals[g] = term if c == 0 else totals[g] + term
        for g in range(GROUP):
            place = jnp.where(codes[g] >= 0, lax.shift_right_arithmetic(codes[g], 1), templates)
            totals_ref[place] += totals[g]

    @pl.when(chunk == pl.num_programs(0) - 1)
    def _():
        rows = keep_ref.shape[2]

        def turn(k, carry):
            left, right = totals_ref[k, :, :LANES], totals_ref[k, :, LANES:]
            stack = [left, ahead(left, LANES // 2), right, ahead(right, LANES // 2)]
            lags = jnp.concatenate(stack, axis=0).T
            turned[...] = lags[: LANES // 2]
            for slot in range(parts):
                piece = lax.bitwise_xor(me_ref[0], slot)
                target = send_ref if slot & 1 else keep_ref
                target[slot >> 1, k] = turned[pl.ds(pl.multiple_of(piece * rows, 8), rows), :]
            return carry

        lax.fori_loop(0, templates, turn, 0)


def correlate(arrived, filters, sources, axis):
    blocks, half, window = arrived.shape
    templates = filters.shape[0]
    taps = filters.shape[2]
    pairs = templates * 2
    lags = window - taps
    parts = lax.axis_size(axis)
    cols = lags // SHIFTS
    assert cols == 2 * LANES and LANES == 4 * SHIFTS
    used = window // LANES
    depth = -(-(taps + SHIFTS) // LANES) * LANES
    lanes = arrived.reshape(blocks, half, used, LANES)
    wide = filters.astype(jnp.float32)
    gain = 1.0 / (taps * jnp.sqrt(jnp.mean(wide * wide, axis=2) + EPSILON))

    named = sources.reshape(pairs)
    ids = jnp.arange(pairs, dtype=jnp.int32)
    edges = jnp.arange(blocks, dtype=jnp.int32)
    counts = jnp.sum((named[None, :] == edges[:, None]).astype(jnp.int32), axis=1)
    chunks = (counts + (GROUP - 1)) >> (GROUP.bit_length() - 1)
    ends = jnp.sum(jnp.where(edges[None, :] <= edges[:, None], chunks[None, :], 0), axis=1)
    begin = jnp.sum(jnp.where(edges[None, :] < named[:, None], chunks[None, :], 0), axis=1)
    same = (named[None, :] == named[:, None]) & (ids[None, :] < ids[:, None])
    place = begin * GROUP + jnp.sum(same.astype(jnp.int32), axis=1)
    steps = (pairs + blocks * (GROUP - 1)) // GROUP
    spots = jnp.arange(steps * GROUP, dtype=jnp.int32)
    order = jnp.sum(jnp.where(place[None, :] == spots[:, None], ids[None, :] + 1, 0), axis=1) - 1
    numbers = jnp.arange(steps, dtype=jnp.int32)
    owner = jnp.sum((ends[None, :] <= numbers[:, None]).astype(jnp.int32), axis=1)
    me = lax.axis_index(axis).astype(jnp.int32).reshape(1)
    smem = pl.BlockSpec(memory_space=pltpu.SMEM)
    skew_shape = (1, half, GROUP * SHIFTS, depth)
    skewed = pl.pallas_call(
        functools.partial(skew_kernel, (half, taps, depth, blocks)),
        grid_spec=pltpu.PrefetchScalarGridSpec(
            num_scalar_prefetch=2,
            grid=(steps,),
            in_specs=[pl.BlockSpec(filters.shape, lambda i, *_: (0, 0, 0))],
            out_specs=pl.BlockSpec(skew_shape, lambda i, *_: (i, 0, 0, 0)),
        ),
        out_shape=jax.ShapeDtypeStruct((steps,) + skew_shape[1:], jnp.bfloat16),
        compiler_params=pltpu.CompilerParams(vmem_limit_bytes=32 * 1024 * 1024),
        cost_estimate=pl.CostEstimate(
            flops=steps * math.prod(skew_shape) * 16,
            bytes_accessed=steps * math.prod(skew_shape) * 2,
            transcendentals=0,
        ),
        name="skew",
    )(owner, order, filters)

    dims = (templates, half, taps, used, parts, blocks)
    piece = (parts // 2, templates, lags // LANES // parts, LANES)
    piece_spec = pl.BlockSpec(piece, lambda i, *_: (0, 0, 0, 0))

    def lanes_at(i, owners, *_):
        return jnp.minimum(owners[i], blocks - 1), 0, 0, 0

    return pl.pallas_call(
        functools.partial(correlate_kernel, dims),
        grid_spec=pltpu.PrefetchScalarGridSpec(
            num_scalar_prefetch=2,
            grid=(steps,),
            in_specs=[
                smem,
                smem,
                pl.BlockSpec((1, half, used, LANES), lanes_at),
                pl.BlockSpec(skew_shape, lambda i, *_: (i, 0, 0, 0)),
            ],
            out_specs=[piece_spec, piece_spec],
            scratch_shapes=[
                pltpu.VMEM((templates + 1, SHIFTS, cols), jnp.float32),
                pltpu.VMEM((LANES, LANES), jnp.float32),
                pltpu.VMEM((half, depth, cols), jnp.bfloat16),
                pltpu.VMEM((half, SHIFTS, cols), jnp.float32),
                pltpu.VMEM((LANES // 2, LANES), jnp.float32),
            ],
        ),
        out_shape=[jax.ShapeDtypeStruct(piece, jnp.float32)] * 2,
        compiler_params=pltpu.CompilerParams(vmem_limit_bytes=32 * 1024 * 1024),
        name="correlate",
    )(owner, order, me, gain.reshape(-1), lanes, skewed)


def swapped(x, axis, bit):
    return lax.ppermute(x, axis, [(i, i ^ bit) for i in range(lax.axis_size(axis))])


def per_device(waveform, templates, block_of, trace_of):
    own_index = lax.axis_index("st")
    station_count = lax.axis_size("st")
    own_templates = templates.shape[0]
    group_chans = templates.shape[1]
    half_chans = group_chans // 2
    window = waveform.shape[2]
    sources = block_of[0].reshape(station_count, own_templates, 2)
    own_sources = lax.dynamic_index_in_dim(sources, own_index, 0, keepdims=False)
    wanted = lax.dynamic_index_in_dim(trace_of[0], own_index, 1, keepdims=False)
    wanted = wanted.reshape(-1)
    station = (wanted * 43691) >> 17
    source_rows = waveform[station, wanted - 3 * station]
    arrived = lax.all_to_all(
        source_rows.reshape(station_count, half_chans, window),
        "st",
        split_axis=0,
        concat_axis=0,
        tiled=True,
    )
    keep, send = correlate(arrived, templates, own_sources, "ch")
    bit = 1
    while True:
        keep = keep + swapped(send, "ch", bit)
        if keep.shape[0] == 1:
            break
        halves = keep.reshape(keep.shape[0] // 2, 2, *keep.shape[1:])
        keep, send = halves[:, 0], halves[:, 1]
        bit *= 2
    return keep.reshape(own_templates, -1)


def solution(mesh):
    in_specs = (
        P("st", None, None),
        P("st", "ch", None),
        P("ch", None, None),
        P("ch", None, None, None),
    )
    out_specs = P("st", "ch")
    return jax.shard_map(
        per_device, mesh=mesh, in_specs=in_specs, out_specs=out_specs, check_vma=False
    )
```

```python
import functools

import jax
import jax.numpy as jnp
from jax import lax
from jax.experimental import pallas as pl
from jax.experimental.pallas import tpu as pltpu
from jax.sharding import PartitionSpec as P

EPSILON = 1e-05
SHIFTS = 32
LANES = 128
GROUP = 4


def correlate_kernel(
    dims,
    me_ref,
    start_ref,
    order_ref,
    gain_ref,
    steps_ref,
    lanes_ref,
    filters_ref,
    keep_ref,
    send_ref,
    totals_ref,
    padded,
    hankel,
    skewed,
    scale,
    turned,
):
    templates, half, taps, used, depth, parts = dims
    block = pl.program_id(0)

    @pl.when(block == 0)
    def _():
        totals_ref[...] = jnp.zeros_like(totals_ref)
        hankel[...] = jnp.zeros_like(hankel)
        padded[...] = jnp.zeros_like(padded)

    low = lax.broadcasted_iota(jnp.int32, (SHIFTS, LANES), 1) < LANES // 2
    whole = taps // LANES
    splits = LANES // SHIFTS

    def ahead(x, by):
        by = (LANES - by) % LANES
        return x if by == 0 else pltpu.roll(x, by, 1)

    def strip(x, m):
        at = (m % splits) * SHIFTS
        return x[at : at + SHIFTS]

    def joined(x, m):
        left = ahead(strip(x, m), m // splits)
        right = ahead(strip(x, m + 1), (m + 1) // splits - LANES // 2)
        return jnp.where(low, left, right)

    for c in range(half):
        padded[:used, :] = lanes_ref[0, c].astype(jnp.float32)
        lanes = padded[...].T
        steps = taps // SHIFTS + 1
        for m in range(steps + 2):
            pair = joined(lanes, m).astype(jnp.bfloat16)
            if m < steps:
                hankel[c, m * SHIFTS : (m + 1) * SHIFTS, :LANES] = pair
            if m >= 2:
                hankel[c, (m - 2) * SHIFTS : (m - 1) * SHIFTS, LANES:] = pair
        squares = lanes * lanes
        high = squares.astype(jnp.bfloat16)
        rest = (squares - high.astype(jnp.float32)).astype(jnp.bfloat16)
        sums = jnp.dot(
            steps_ref[...],
            jnp.concatenate([high, rest], axis=1),
            preferred_element_type=jnp.float32,
        )
        sums = sums[:, :LANES] + sums[:, LANES:]
        before, suffix = sums[:LANES], sums[LANES:]
        total = suffix[0:1]
        middle = jnp.zeros_like(total)
        for by in range(1, whole):
            middle = middle + ahead(total, by)
        energy = suffix + middle + ahead(before, whole)
        root = lax.rsqrt(energy / taps + EPSILON)
        scale[c, :, :LANES] = joined(root, 0)
        scale[c, :, LANES:] = joined(root, 2)

    first, last = start_ref[block], start_ref[block + 1]

    def chunk(number, carry):
        base = first + number * GROUP
        for g in range(GROUP):
            pair = order_ref[base + g]
            rows = filters_ref[pair]
            for c in range(half):
                spread = jnp.broadcast_to(rows[c : c + 1], (SHIFTS, depth))
                spread = pltpu.roll(spread, 0, 1, stride=1, stride_axis=0)
                skewed[c, g * SHIFTS : (g + 1) * SHIFTS, :] = spread.astype(jnp.bfloat16)
        totals = [None] * GROUP
        for c in range(half):
            raw = jnp.dot(skewed[c], hankel[c], preferred_element_type=jnp.float32)
            for g in range(GROUP):
                pair = order_ref[base + g]
                term = raw[g * SHIFTS : (g + 1) * SHIFTS] * (scale[c] * gain_ref[pair * half + c])
                totals[g] = term if c == 0 else totals[g] + term
        for g in range(GROUP):
            place = jnp.where(base + g < last, lax.div(order_ref[base + g], 2), templates)
            totals_ref[place] += totals[g]
        return carry

    lax.fori_loop(0, lax.div(last - first + GROUP - 1, GROUP), chunk, 0)

    @pl.when(block == pl.num_programs(0) - 1)
    def _():
        rows = keep_ref.shape[2]

        def turn(k, carry):
            left, right = totals_ref[k, :, :LANES], totals_ref[k, :, LANES:]
            stack = [left, ahead(left, LANES // 2), right, ahead(right, LANES // 2)]
            lags = jnp.concatenate(stack, axis=0).T
            turned[...] = lags[: LANES // 2]
            for slot in range(parts):
                piece = lax.bitwise_xor(me_ref[0], slot)
                target = send_ref if slot & 1 else keep_ref
                target[slot >> 1, k] = turned[pl.ds(pl.multiple_of(piece * rows, 8), rows), :]
            return carry

        lax.fori_loop(0, templates, turn, 0)


def correlate(arrived, filters, sources, axis):
    blocks, half, window = arrived.shape
    templates = filters.shape[0]
    taps = filters.shape[2]
    pairs = templates * 2
    lags = window - taps
    parts = lax.axis_size(axis)
    cols = lags // SHIFTS
    assert cols == 2 * LANES and LANES == 4 * SHIFTS
    used = window // LANES
    depth = -(-(taps + SHIFTS) // LANES) * LANES
    lanes = arrived.reshape(blocks, half, used, LANES)
    wide = filters.astype(jnp.float32)
    gain = 1.0 / (taps * jnp.sqrt(jnp.mean(wide * wide, axis=2) + EPSILON))
    padded = jnp.pad(wide.reshape(pairs, half, taps), ((0, 0), (0, 0), (0, depth - taps)))

    named = sources.reshape(pairs)
    ids = jnp.arange(pairs, dtype=jnp.int32)
    ahead = (named[None, :] < named[:, None]) | (
        (named[None, :] == named[:, None]) & (ids[None, :] < ids[:, None])
    )
    place = jnp.sum(ahead.astype(jnp.int32), axis=1)
    spots = jnp.arange(pairs + GROUP, dtype=jnp.int32)
    order = jnp.sum(jnp.where(place[None, :] == spots[:, None], ids[None, :], 0), axis=1)
    edges = jnp.arange(blocks + 1, dtype=jnp.int32)
    start = jnp.sum((named[None, :] < edges[:, None]).astype(jnp.int32), axis=1)

    spots = jnp.arange(LANES)
    earlier = spots[None, :] < spots[:, None]
    steps = jnp.concatenate([earlier, ~earlier], axis=0).astype(jnp.bfloat16)
    me = lax.axis_index(axis).astype(jnp.int32).reshape(1)
    dims = (templates, half, taps, used, depth, parts)
    smem = pl.BlockSpec(memory_space=pltpu.SMEM)
    piece = (parts // 2, templates, lags // LANES // parts, LANES)
    piece_spec = pl.BlockSpec(piece, lambda b: (0, 0, 0, 0))
    return pl.pallas_call(
        functools.partial(correlate_kernel, dims),
        grid=(blocks,),
        out_shape=[jax.ShapeDtypeStruct(piece, jnp.float32)] * 2,
        in_specs=[
            smem,
            smem,
            smem,
            smem,
            pl.BlockSpec((2 * LANES, LANES), lambda b: (0, 0)),
            pl.BlockSpec((1, half, used, LANES), lambda b: (b, 0, 0, 0)),
            pl.BlockSpec((pairs, half, depth), lambda b: (0, 0, 0)),
        ],
        out_specs=[piece_spec, piece_spec],
        scratch_shapes=[
            pltpu.VMEM((templates + 1, SHIFTS, cols), jnp.float32),
            pltpu.VMEM((LANES, LANES), jnp.float32),
            pltpu.VMEM((half, depth, cols), jnp.bfloat16),
            pltpu.VMEM((half, GROUP * SHIFTS, depth), jnp.bfloat16),
            pltpu.VMEM((half, SHIFTS, cols), jnp.float32),
            pltpu.VMEM((LANES // 2, LANES), jnp.float32),
        ],
        compiler_params=pltpu.CompilerParams(vmem_limit_bytes=40 * 1024 * 1024),
        name="correlate",
    )(me, start, order, gain.reshape(-1), steps, lanes, padded)


def swapped(x, axis, bit):
    return lax.ppermute(x, axis, [(i, i ^ bit) for i in range(lax.axis_size(axis))])


def per_device(waveform, templates, block_of, trace_of):
    own_index = lax.axis_index("st")
    station_count = lax.axis_size("st")
    own_templates = templates.shape[0]
    group_chans = templates.shape[1]
    half_chans = group_chans // 2
    window = waveform.shape[2]
    sources = block_of[0].reshape(station_count, own_templates, 2)
    own_sources = lax.dynamic_index_in_dim(sources, own_index, 0, keepdims=False)
    wanted = lax.dynamic_index_in_dim(trace_of[0], own_index, 1, keepdims=False)
    wanted = wanted.reshape(-1)
    station = (wanted * 43691) >> 17
    source_rows = waveform[station, wanted - 3 * station]
    arrived = lax.all_to_all(
        source_rows.reshape(station_count, half_chans, window),
        "st",
        split_axis=0,
        concat_axis=0,
        tiled=True,
    )
    keep, send = correlate(arrived, templates, own_sources, "ch")
    bit = 1
    while True:
        keep = keep + swapped(send, "ch", bit)
        if keep.shape[0] == 1:
            break
        halves = keep.reshape(keep.shape[0] // 2, 2, *keep.shape[1:])
        keep, send = halves[:, 0], halves[:, 1]
        bit *= 2
    return keep.reshape(own_templates, -1)


def solution(mesh):
    in_specs = (
        P("st", None, None),
        P("st", "ch", None),
        P("ch", None, None),
        P("ch", None, None, None),
    )
    out_specs = P("st", "ch")
    return jax.shard_map(
        per_device, mesh=mesh, in_specs=in_specs, out_specs=out_specs, check_vma=False
    )
```

```python
import functools

import jax
import jax.numpy as jnp
from jax import lax
from jax.experimental import pallas as pl
from jax.experimental.pallas import tpu as pltpu
from jax.sharding import PartitionSpec as P

EPSILON = 1e-05
SHIFTS = 32
LANES = 128
GROUP = 8


def correlate_kernel(
    dims,
    me_ref,
    start_ref,
    order_ref,
    gain_ref,
    steps_ref,
    lanes_ref,
    filters_ref,
    keep_ref,
    send_ref,
    totals_ref,
    padded,
    hankel,
    skewed,
    scale,
    turned,
):
    templates, half, taps, used, depth, parts = dims
    block = pl.program_id(0)

    @pl.when(block == 0)
    def _():
        totals_ref[...] = jnp.zeros_like(totals_ref)
        hankel[...] = jnp.zeros_like(hankel)
        padded[...] = jnp.zeros_like(padded)

    low = lax.broadcasted_iota(jnp.int32, (SHIFTS, LANES), 1) < LANES // 2
    whole = taps // LANES
    splits = LANES // SHIFTS

    def ahead(x, by):
        by = (LANES - by) % LANES
        return x if by == 0 else pltpu.roll(x, by, 1)

    def strip(x, m):
        at = (m % splits) * SHIFTS
        return x[at : at + SHIFTS]

    def joined(x, m):
        left = ahead(strip(x, m), m // splits)
        right = ahead(strip(x, m + 1), (m + 1) // splits - LANES // 2)
        return jnp.where(low, left, right)

    for c in range(half):
        padded[:used, :] = lanes_ref[0, c].astype(jnp.float32)
        lanes = padded[...].T
        steps = taps // SHIFTS + 1
        for m in range(steps + 2):
            pair = joined(lanes, m).astype(jnp.bfloat16)
            if m < steps:
                hankel[c, m * SHIFTS : (m + 1) * SHIFTS, :LANES] = pair
            if m >= 2:
                hankel[c, (m - 2) * SHIFTS : (m - 1) * SHIFTS, LANES:] = pair
        squares = lanes * lanes
        high = squares.astype(jnp.bfloat16)
        rest = (squares - high.astype(jnp.float32)).astype(jnp.bfloat16)
        sums = jnp.dot(
            steps_ref[...],
            jnp.concatenate([high, rest], axis=1),
            preferred_element_type=jnp.float32,
        )
        sums = sums[:, :LANES] + sums[:, LANES:]
        before, suffix = sums[:LANES], sums[LANES:]
        total = suffix[0:1]
        middle = jnp.zeros_like(total)
        for by in range(1, whole):
            middle = middle + ahead(total, by)
        energy = suffix + middle + ahead(before, whole)
        root = lax.rsqrt(energy / taps + EPSILON)
        scale[c, :, :LANES] = joined(root, 0)
        scale[c, :, LANES:] = joined(root, 2)

    first, last = start_ref[block], start_ref[block + 1]

    def chunk(number, carry):
        base = first + number * GROUP
        for g in range(GROUP):
            pair = order_ref[base + g]
            rows = filters_ref[pair]
            for c in range(half):
                spread = jnp.broadcast_to(rows[c : c + 1], (SHIFTS, depth))
                spread = pltpu.roll(spread, 0, 1, stride=1, stride_axis=0)
                skewed[c, g * SHIFTS : (g + 1) * SHIFTS, :] = spread.astype(jnp.bfloat16)
        totals = [None] * GROUP
        for c in range(half):
            raw = jnp.dot(skewed[c], hankel[c], preferred_element_type=jnp.float32)
            for g in range(GROUP):
                pair = order_ref[base + g]
                term = raw[g * SHIFTS : (g + 1) * SHIFTS] * (scale[c] * gain_ref[pair * half + c])
                totals[g] = term if c == 0 else totals[g] + term
        for g in range(GROUP):
            place = jnp.where(base + g < last, lax.div(order_ref[base + g], 2), templates)
            totals_ref[place] += totals[g]
        return carry

    lax.fori_loop(0, lax.div(last - first + GROUP - 1, GROUP), chunk, 0)

    @pl.when(block == pl.num_programs(0) - 1)
    def _():
        rows = keep_ref.shape[2]

        def turn(k, carry):
            left, right = totals_ref[k, :, :LANES], totals_ref[k, :, LANES:]
            stack = [left, ahead(left, LANES // 2), right, ahead(right, LANES // 2)]
            lags = jnp.concatenate(stack, axis=0).T
            turned[...] = lags[: LANES // 2]
            for slot in range(parts):
                piece = lax.bitwise_xor(me_ref[0], slot)
                target = send_ref if slot & 1 else keep_ref
                target[slot >> 1, k] = turned[pl.ds(pl.multiple_of(piece * rows, 8), rows), :]
            return carry

        lax.fori_loop(0, templates, turn, 0)


def correlate(arrived, filters, sources, axis):
    blocks, half, window = arrived.shape
    templates = filters.shape[0]
    taps = filters.shape[2]
    pairs = templates * 2
    lags = window - taps
    parts = lax.axis_size(axis)
    cols = lags // SHIFTS
    assert cols == 2 * LANES and LANES == 4 * SHIFTS
    used = window // LANES
    depth = -(-(taps + SHIFTS) // LANES) * LANES
    lanes = arrived.reshape(blocks, half, used, LANES)
    wide = filters.astype(jnp.float32)
    gain = 1.0 / (taps * jnp.sqrt(jnp.mean(wide * wide, axis=2) + EPSILON))
    padded = jnp.pad(wide.reshape(pairs, half, taps), ((0, 0), (0, 0), (0, depth - taps)))

    named = sources.reshape(pairs)
    ids = jnp.arange(pairs, dtype=jnp.int32)
    ahead = (named[None, :] < named[:, None]) | (
        (named[None, :] == named[:, None]) & (ids[None, :] < ids[:, None])
    )
    place = jnp.sum(ahead.astype(jnp.int32), axis=1)
    spots = jnp.arange(pairs + GROUP, dtype=jnp.int32)
    order = jnp.sum(jnp.where(place[None, :] == spots[:, None], ids[None, :], 0), axis=1)
    edges = jnp.arange(blocks + 1, dtype=jnp.int32)
    start = jnp.sum((named[None, :] < edges[:, None]).astype(jnp.int32), axis=1)

    spots = jnp.arange(LANES)
    earlier = spots[None, :] < spots[:, None]
    steps = jnp.concatenate([earlier, ~earlier], axis=0).astype(jnp.bfloat16)
    me = lax.axis_index(axis).astype(jnp.int32).reshape(1)
    dims = (templates, half, taps, used, depth, parts)
    smem = pl.BlockSpec(memory_space=pltpu.SMEM)
    piece = (parts // 2, templates, lags // LANES // parts, LANES)
    piece_spec = pl.BlockSpec(piece, lambda b: (0, 0, 0, 0))
    return pl.pallas_call(
        functools.partial(correlate_kernel, dims),
        grid=(blocks,),
        out_shape=[jax.ShapeDtypeStruct(piece, jnp.float32)] * 2,
        in_specs=[
            smem,
            smem,
            smem,
            smem,
            pl.BlockSpec((2 * LANES, LANES), lambda b: (0, 0)),
            pl.BlockSpec((1, half, used, LANES), lambda b: (b, 0, 0, 0)),
            pl.BlockSpec((pairs, half, depth), lambda b: (0, 0, 0)),
        ],
        out_specs=[piece_spec, piece_spec],
        scratch_shapes=[
            pltpu.VMEM((templates + 1, SHIFTS, cols), jnp.float32),
            pltpu.VMEM((LANES, LANES), jnp.float32),
            pltpu.VMEM((half, depth, cols), jnp.bfloat16),
            pltpu.VMEM((half, GROUP * SHIFTS, depth), jnp.bfloat16),
            pltpu.VMEM((half, SHIFTS, cols), jnp.float32),
            pltpu.VMEM((LANES // 2, LANES), jnp.float32),
        ],
        compiler_params=pltpu.CompilerParams(vmem_limit_bytes=40 * 1024 * 1024),
        name="correlate",
    )(me, start, order, gain.reshape(-1), steps, lanes, padded)


def swapped(x, axis, bit):
    return lax.ppermute(x, axis, [(i, i ^ bit) for i in range(lax.axis_size(axis))])


def per_device(waveform, templates, block_of, trace_of):
    own_index = lax.axis_index("st")
    station_count = lax.axis_size("st")
    own_templates = templates.shape[0]
    group_chans = templates.shape[1]
    half_chans = group_chans // 2
    window = waveform.shape[2]
    sources = block_of[0].reshape(station_count, own_templates, 2)
    own_sources = lax.dynamic_index_in_dim(sources, own_index, 0, keepdims=False)
    wanted = lax.dynamic_index_in_dim(trace_of[0], own_index, 1, keepdims=False)
    wanted = wanted.reshape(-1)
    station = (wanted * 43691) >> 17
    source_rows = waveform[station, wanted - 3 * station]
    arrived = lax.all_to_all(
        source_rows.reshape(station_count, half_chans, window),
        "st",
        split_axis=0,
        concat_axis=0,
        tiled=True,
    )
    keep, send = correlate(arrived, templates, own_sources, "ch")
    bit = 1
    while True:
        keep = keep + swapped(send, "ch", bit)
        if keep.shape[0] == 1:
            break
        halves = keep.reshape(keep.shape[0] // 2, 2, *keep.shape[1:])
        keep, send = halves[:, 0], halves[:, 1]
        bit *= 2
    return keep.reshape(own_templates, -1)


def solution(mesh):
    in_specs = (
        P("st", None, None),
        P("st", "ch", None),
        P("ch", None, None),
        P("ch", None, None, None),
    )
    out_specs = P("st", "ch")
    return jax.shard_map(
        per_device, mesh=mesh, in_specs=in_specs, out_specs=out_specs, check_vma=False
    )
```

```python
import functools

import jax
import jax.numpy as jnp
from jax import lax
from jax.experimental import pallas as pl
from jax.experimental.pallas import tpu as pltpu
from jax.sharding import PartitionSpec as P

EPSILON = 1e-05
SHIFTS = 32
LANES = 128
GROUP = 17


def correlate_kernel(
    dims,
    me_ref,
    start_ref,
    order_ref,
    gain_ref,
    steps_ref,
    lanes_ref,
    filters_ref,
    keep_ref,
    send_ref,
    totals_ref,
    padded,
    hankel,
    skewed,
    scale,
    turned,
):
    templates, half, taps, used, depth, parts = dims
    block = pl.program_id(0)

    @pl.when(block == 0)
    def _():
        totals_ref[...] = jnp.zeros_like(totals_ref)
        hankel[...] = jnp.zeros_like(hankel)
        padded[...] = jnp.zeros_like(padded)

    low = lax.broadcasted_iota(jnp.int32, (SHIFTS, LANES), 1) < LANES // 2
    whole = taps // LANES
    splits = LANES // SHIFTS

    def ahead(x, by):
        by = (LANES - by) % LANES
        return x if by == 0 else pltpu.roll(x, by, 1)

    def strip(x, m):
        at = (m % splits) * SHIFTS
        return x[at : at + SHIFTS]

    def joined(x, m):
        left = ahead(strip(x, m), m // splits)
        right = ahead(strip(x, m + 1), (m + 1) // splits - LANES // 2)
        return jnp.where(low, left, right)

    for c in range(half):
        padded[:used, :] = lanes_ref[0, c].astype(jnp.float32)
        lanes = padded[...].T
        steps = taps // SHIFTS + 1
        for m in range(steps + 2):
            pair = joined(lanes, m).astype(jnp.bfloat16)
            if m < steps:
                hankel[c, m * SHIFTS : (m + 1) * SHIFTS, :LANES] = pair
            if m >= 2:
                hankel[c, (m - 2) * SHIFTS : (m - 1) * SHIFTS, LANES:] = pair
        squares = lanes * lanes
        high = squares.astype(jnp.bfloat16)
        rest = (squares - high.astype(jnp.float32)).astype(jnp.bfloat16)
        sums = jnp.dot(
            steps_ref[...],
            jnp.concatenate([high, rest], axis=1),
            preferred_element_type=jnp.float32,
        )
        sums = sums[:, :LANES] + sums[:, LANES:]
        before, suffix = sums[:LANES], sums[LANES:]
        total = suffix[0:1]
        middle = jnp.zeros_like(total)
        for by in range(1, whole):
            middle = middle + ahead(total, by)
        energy = suffix + middle + ahead(before, whole)
        root = lax.rsqrt(energy / taps + EPSILON)
        scale[c, :, :LANES] = joined(root, 0)
        scale[c, :, LANES:] = joined(root, 2)

    first, last = start_ref[block], start_ref[block + 1]

    def chunk(number, carry):
        base = first + number * GROUP
        for g in range(GROUP):
            pair = order_ref[base + g]
            rows = filters_ref[pair]
            for c in range(half):
                spread = jnp.broadcast_to(rows[c : c + 1], (SHIFTS, depth))
                spread = pltpu.roll(spread, 0, 1, stride=1, stride_axis=0)
                skewed[c, g * SHIFTS : (g + 1) * SHIFTS, :] = spread.astype(jnp.bfloat16)
        totals = [None] * GROUP
        for c in range(half):
            raw = jnp.dot(skewed[c], hankel[c], preferred_element_type=jnp.float32)
            for g in range(GROUP):
                pair = order_ref[base + g]
                term = raw[g * SHIFTS : (g + 1) * SHIFTS] * (scale[c] * gain_ref[pair * half + c])
                totals[g] = term if c == 0 else totals[g] + term
        for g in range(GROUP):
            place = jnp.where(base + g < last, lax.div(order_ref[base + g], 2), templates)
            totals_ref[place] += totals[g]
        return carry

    lax.fori_loop(0, lax.div(last - first + GROUP - 1, GROUP), chunk, 0)

    @pl.when(block == pl.num_programs(0) - 1)
    def _():
        rows = keep_ref.shape[2]

        def turn(k, carry):
            left, right = totals_ref[k, :, :LANES], totals_ref[k, :, LANES:]
            stack = [left, ahead(left, LANES // 2), right, ahead(right, LANES // 2)]
            lags = jnp.concatenate(stack, axis=0).T
            turned[...] = lags[: LANES // 2]
            for slot in range(parts):
                piece = lax.bitwise_xor(me_ref[0], slot)
                target = send_ref if slot & 1 else keep_ref
                target[slot >> 1, k] = turned[pl.ds(pl.multiple_of(piece * rows, 8), rows), :]
            return carry

        lax.fori_loop(0, templates, turn, 0)


def correlate(arrived, filters, sources, axis):
    blocks, half, window = arrived.shape
    templates = filters.shape[0]
    taps = filters.shape[2]
    pairs = templates * 2
    lags = window - taps
    parts = lax.axis_size(axis)
    cols = lags // SHIFTS
    assert cols == 2 * LANES and LANES == 4 * SHIFTS
    used = window // LANES
    depth = -(-(taps + SHIFTS) // LANES) * LANES
    lanes = arrived.reshape(blocks, half, used, LANES)
    wide = filters.astype(jnp.float32)
    gain = 1.0 / (taps * jnp.sqrt(jnp.mean(wide * wide, axis=2) + EPSILON))
    padded = jnp.pad(wide.reshape(pairs, half, taps), ((0, 0), (0, 0), (0, depth - taps)))

    named = sources.reshape(pairs)
    ids = jnp.arange(pairs, dtype=jnp.int32)
    ahead = (named[None, :] < named[:, None]) | (
        (named[None, :] == named[:, None]) & (ids[None, :] < ids[:, None])
    )
    place = jnp.sum(ahead.astype(jnp.int32), axis=1)
    spots = jnp.arange(pairs + GROUP, dtype=jnp.int32)
    order = jnp.sum(jnp.where(place[None, :] == spots[:, None], ids[None, :], 0), axis=1)
    edges = jnp.arange(blocks + 1, dtype=jnp.int32)
    start = jnp.sum((named[None, :] < edges[:, None]).astype(jnp.int32), axis=1)

    spots = jnp.arange(LANES)
    earlier = spots[None, :] < spots[:, None]
    steps = jnp.concatenate([earlier, ~earlier], axis=0).astype(jnp.bfloat16)
    me = lax.axis_index(axis).astype(jnp.int32).reshape(1)
    dims = (templates, half, taps, used, depth, parts)
    smem = pl.BlockSpec(memory_space=pltpu.SMEM)
    piece = (parts // 2, templates, lags // LANES // parts, LANES)
    piece_spec = pl.BlockSpec(piece, lambda b: (0, 0, 0, 0))
    return pl.pallas_call(
        functools.partial(correlate_kernel, dims),
        grid=(blocks,),
        out_shape=[jax.ShapeDtypeStruct(piece, jnp.float32)] * 2,
        in_specs=[
            smem,
            smem,
            smem,
            smem,
            pl.BlockSpec((2 * LANES, LANES), lambda b: (0, 0)),
            pl.BlockSpec((1, half, used, LANES), lambda b: (b, 0, 0, 0)),
            pl.BlockSpec((pairs, half, depth), lambda b: (0, 0, 0)),
        ],
        out_specs=[piece_spec, piece_spec],
        scratch_shapes=[
            pltpu.VMEM((templates + 1, SHIFTS, cols), jnp.float32),
            pltpu.VMEM((LANES, LANES), jnp.float32),
            pltpu.VMEM((half, depth, cols), jnp.bfloat16),
            pltpu.VMEM((half, GROUP * SHIFTS, depth), jnp.bfloat16),
            pltpu.VMEM((half, SHIFTS, cols), jnp.float32),
            pltpu.VMEM((LANES // 2, LANES), jnp.float32),
        ],
        compiler_params=pltpu.CompilerParams(vmem_limit_bytes=40 * 1024 * 1024),
        name="correlate",
    )(me, start, order, gain.reshape(-1), steps, lanes, padded)


def swapped(x, axis, bit):
    return lax.ppermute(x, axis, [(i, i ^ bit) for i in range(lax.axis_size(axis))])


def per_device(waveform, templates, block_of, trace_of):
    own_index = lax.axis_index("st")
    station_count = lax.axis_size("st")
    own_templates = templates.shape[0]
    group_chans = templates.shape[1]
    half_chans = group_chans // 2
    window = waveform.shape[2]
    sources = block_of[0].reshape(station_count, own_templates, 2)
    own_sources = lax.dynamic_index_in_dim(sources, own_index, 0, keepdims=False)
    wanted = lax.dynamic_index_in_dim(trace_of[0], own_index, 1, keepdims=False)
    wanted = wanted.reshape(-1)
    station = (wanted * 43691) >> 17
    source_rows = waveform[station, wanted - 3 * station]
    arrived = lax.all_to_all(
        source_rows.reshape(station_count, half_chans, window),
        "st",
        split_axis=0,
        concat_axis=0,
        tiled=True,
    )
    keep, send = correlate(arrived, templates, own_sources, "ch")
    bit = 1
    while True:
        keep = keep + swapped(send, "ch", bit)
        if keep.shape[0] == 1:
            break
        halves = keep.reshape(keep.shape[0] // 2, 2, *keep.shape[1:])
        keep, send = halves[:, 0], halves[:, 1]
        bit *= 2
    return keep.reshape(own_templates, -1)


def solution(mesh):
    in_specs = (
        P("st", None, None),
        P("st", "ch", None),
        P("ch", None, None),
        P("ch", None, None, None),
    )
    out_specs = P("st", "ch")
    return jax.shard_map(
        per_device, mesh=mesh, in_specs=in_specs, out_specs=out_specs, check_vma=False
    )
```

```python
import functools
import math

import jax
import jax.numpy as jnp
from jax import lax
from jax.experimental import pallas as pl
from jax.experimental.pallas import tpu as pltpu
from jax.sharding import PartitionSpec as P

EPSILON = 1e-05
SHIFTS = 32
LANES = 128
GROUP = 17


def correlate_kernel(
    dims,
    me_ref,
    start_ref,
    order_ref,
    gain_ref,
    steps_ref,
    lanes_ref,
    filters_ref,
    keep_ref,
    send_ref,
    totals_ref,
    padded,
    hankel,
    skewed,
    scale,
    turned,
):
    templates, half, taps, used, depth, parts = dims
    block = pl.program_id(0)

    @pl.when(block == 0)
    def _():
        totals_ref[...] = jnp.zeros_like(totals_ref)
        hankel[...] = jnp.zeros_like(hankel)
        padded[...] = jnp.zeros_like(padded)

    low = lax.broadcasted_iota(jnp.int32, (SHIFTS, LANES), 1) < LANES // 2
    whole = taps // LANES
    splits = LANES // SHIFTS

    def ahead(x, by):
        by = (LANES - by) % LANES
        return x if by == 0 else pltpu.roll(x, by, 1)

    def strip(x, m):
        at = (m % splits) * SHIFTS
        return x[at : at + SHIFTS]

    def joined(x, m):
        left = ahead(strip(x, m), m // splits)
        right = ahead(strip(x, m + 1), (m + 1) // splits - LANES // 2)
        return jnp.where(low, left, right)

    for c in range(half):
        padded[:used, :] = lanes_ref[0, c].astype(jnp.float32)
        lanes = padded[...].T
        steps = taps // SHIFTS + 1
        for m in range(steps + 2):
            pair = joined(lanes, m).astype(jnp.bfloat16)
            if m < steps:
                hankel[c, m * SHIFTS : (m + 1) * SHIFTS, :LANES] = pair
            if m >= 2:
                hankel[c, (m - 2) * SHIFTS : (m - 1) * SHIFTS, LANES:] = pair
        squares = lanes * lanes
        high = squares.astype(jnp.bfloat16)
        rest = (squares - high.astype(jnp.float32)).astype(jnp.bfloat16)
        sums = jnp.dot(
            steps_ref[...],
            jnp.concatenate([high, rest], axis=1),
            preferred_element_type=jnp.float32,
        )
        sums = sums[:, :LANES] + sums[:, LANES:]
        before, suffix = sums[:LANES], sums[LANES:]
        total = suffix[0:1]
        middle = jnp.zeros_like(total)
        for by in range(1, whole):
            middle = middle + ahead(total, by)
        energy = suffix + middle + ahead(before, whole)
        root = lax.rsqrt(energy / taps + EPSILON)
        scale[c, :, :LANES] = joined(root, 0)
        scale[c, :, LANES:] = joined(root, 2)

    first, last = start_ref[block], start_ref[block + 1]

    def chunk(number, carry):
        base = first + number * GROUP
        for g in range(GROUP):
            pair = order_ref[base + g]
            rows = filters_ref[pair]
            for c in range(half):
                spread = jnp.broadcast_to(rows[c : c + 1], (SHIFTS, depth))
                spread = pltpu.roll(spread, 0, 1, stride=1, stride_axis=0)
                skewed[c, g * SHIFTS : (g + 1) * SHIFTS, :] = spread.astype(jnp.bfloat16)
        totals = [None] * GROUP
        for c in range(half):
            raw = jnp.dot(skewed[c], hankel[c], preferred_element_type=jnp.float32)
            for g in range(GROUP):
                pair = order_ref[base + g]
                term = raw[g * SHIFTS : (g + 1) * SHIFTS] * (scale[c] * gain_ref[pair * half + c])
                totals[g] = term if c == 0 else totals[g] + term
        for g in range(GROUP):
            place = jnp.where(base + g < last, lax.div(order_ref[base + g], 2), templates)
            totals_ref[place] += totals[g]
        return carry

    lax.fori_loop(0, lax.div(last - first + GROUP - 1, GROUP), chunk, 0)

    @pl.when(block == pl.num_programs(0) - 1)
    def _():
        rows = keep_ref.shape[2]

        batch = turned.shape[0]

        def turn(number, carry):
            for j in range(batch):
                k = number * batch + j
                left, right = totals_ref[k, :, :LANES], totals_ref[k, :, LANES:]
                stack = [left, ahead(left, LANES // 2), right, ahead(right, LANES // 2)]
                turned[j] = jnp.concatenate(stack, axis=0).T[: LANES // 2]
            for slot in range(parts):
                piece = lax.bitwise_xor(me_ref[0], slot)
                at = pl.ds(pl.multiple_of(piece * rows, 8), rows)
                target = send_ref if slot & 1 else keep_ref
                for j in range(batch):
                    target[slot >> 1, number * batch + j] = turned[j, at, :]
            return carry

        lax.fori_loop(0, templates // batch, turn, 0)


def correlate(arrived, filters, sources, axis):
    blocks, half, window = arrived.shape
    templates = filters.shape[0]
    taps = filters.shape[2]
    pairs = templates * 2
    lags = window - taps
    parts = lax.axis_size(axis)
    cols = lags // SHIFTS
    assert cols == 2 * LANES and LANES == 4 * SHIFTS
    used = window // LANES
    depth = -(-(taps + SHIFTS) // LANES) * LANES
    lanes = arrived.reshape(blocks, half, used, LANES)
    wide = filters.astype(jnp.float32)
    gain = 1.0 / (taps * jnp.sqrt(jnp.mean(wide * wide, axis=2) + EPSILON))
    padded = jnp.pad(wide.reshape(pairs, half, taps), ((0, 0), (0, 0), (0, depth - taps)))

    named = sources.reshape(pairs)
    ids = jnp.arange(pairs, dtype=jnp.int32)
    ahead = (named[None, :] < named[:, None]) | (
        (named[None, :] == named[:, None]) & (ids[None, :] < ids[:, None])
    )
    place = jnp.sum(ahead.astype(jnp.int32), axis=1)
    spots = jnp.arange(pairs + GROUP, dtype=jnp.int32)
    order = jnp.sum(jnp.where(place[None, :] == spots[:, None], ids[None, :], 0), axis=1)
    edges = jnp.arange(blocks + 1, dtype=jnp.int32)
    start = jnp.sum((named[None, :] < edges[:, None]).astype(jnp.int32), axis=1)

    spots = jnp.arange(LANES)
    earlier = spots[None, :] < spots[:, None]
    steps = jnp.concatenate([earlier, ~earlier], axis=0).astype(jnp.bfloat16)
    me = lax.axis_index(axis).astype(jnp.int32).reshape(1)
    dims = (templates, half, taps, used, depth, parts)
    smem = pl.BlockSpec(memory_space=pltpu.SMEM)
    piece = (parts // 2, templates, lags // LANES // parts, LANES)
    piece_spec = pl.BlockSpec(piece, lambda b: (0, 0, 0, 0))
    return pl.pallas_call(
        functools.partial(correlate_kernel, dims),
        grid=(blocks,),
        out_shape=[jax.ShapeDtypeStruct(piece, jnp.float32)] * 2,
        in_specs=[
            smem,
            smem,
            smem,
            smem,
            pl.BlockSpec((2 * LANES, LANES), lambda b: (0, 0)),
            pl.BlockSpec((1, half, used, LANES), lambda b: (b, 0, 0, 0)),
            pl.BlockSpec((pairs, half, depth), lambda b: (0, 0, 0)),
        ],
        out_specs=[piece_spec, piece_spec],
        scratch_shapes=[
            pltpu.VMEM((templates + 1, SHIFTS, cols), jnp.float32),
            pltpu.VMEM((LANES, LANES), jnp.float32),
            pltpu.VMEM((half, depth, cols), jnp.bfloat16),
            pltpu.VMEM((half, GROUP * SHIFTS, depth), jnp.bfloat16),
            pltpu.VMEM((half, SHIFTS, cols), jnp.float32),
            pltpu.VMEM((math.gcd(templates, 4), LANES // 2, LANES), jnp.float32),
        ],
        compiler_params=pltpu.CompilerParams(vmem_limit_bytes=40 * 1024 * 1024),
        name="correlate",
    )(me, start, order, gain.reshape(-1), steps, lanes, padded)


def swapped(x, axis, bit):
    return lax.ppermute(x, axis, [(i, i ^ bit) for i in range(lax.axis_size(axis))])


def per_device(waveform, templates, block_of, trace_of):
    own_index = lax.axis_index("st")
    station_count = lax.axis_size("st")
    own_templates = templates.shape[0]
    group_chans = templates.shape[1]
    half_chans = group_chans // 2
    window = waveform.shape[2]
    sources = block_of[0].reshape(station_count, own_templates, 2)
    own_sources = lax.dynamic_index_in_dim(sources, own_index, 0, keepdims=False)
    wanted = lax.dynamic_index_in_dim(trace_of[0], own_index, 1, keepdims=False)
    wanted = wanted.reshape(-1)
    station = (wanted * 43691) >> 17
    source_rows = waveform[station, wanted - 3 * station]
    arrived = lax.all_to_all(
        source_rows.reshape(station_count, half_chans, window),
        "st",
        split_axis=0,
        concat_axis=0,
        tiled=True,
    )
    keep, send = correlate(arrived, templates, own_sources, "ch")
    bit = 1
    while True:
        keep = keep + swapped(send, "ch", bit)
        if keep.shape[0] == 1:
            break
        halves = keep.reshape(keep.shape[0] // 2, 2, *keep.shape[1:])
        keep, send = halves[:, 0], halves[:, 1]
        bit *= 2
    return keep.reshape(own_templates, -1)


def solution(mesh):
    in_specs = (
        P("st", None, None),
        P("st", "ch", None),
        P("ch", None, None),
        P("ch", None, None, None),
    )
    out_specs = P("st", "ch")
    return jax.shard_map(
        per_device, mesh=mesh, in_specs=in_specs, out_specs=out_specs, check_vma=False
    )
```

```python
import functools
import math

import jax
import jax.numpy as jnp
from jax import lax
from jax.experimental import pallas as pl
from jax.experimental.pallas import tpu as pltpu
from jax.sharding import PartitionSpec as P

EPSILON = 1e-05
SHIFTS = 32
LANES = 128
GROUP = 17


def correlate_kernel(
    dims,
    me_ref,
    start_ref,
    order_ref,
    gain_ref,
    steps_ref,
    lanes_ref,
    filters_ref,
    keep_ref,
    send_ref,
    totals_ref,
    padded,
    hankel,
    skewed,
    scale,
    turned,
):
    templates, half, taps, used, depth, parts = dims
    block = pl.program_id(0)

    @pl.when(block == 0)
    def _():
        totals_ref[...] = jnp.zeros_like(totals_ref)
        hankel[...] = jnp.zeros_like(hankel)
        padded[...] = jnp.zeros_like(padded)

    low = lax.broadcasted_iota(jnp.int32, (SHIFTS, LANES), 1) < LANES // 2
    whole = taps // LANES
    splits = LANES // SHIFTS

    def ahead(x, by):
        by = (LANES - by) % LANES
        return x if by == 0 else pltpu.roll(x, by, 1)

    def strip(x, m):
        at = (m % splits) * SHIFTS
        return x[at : at + SHIFTS]

    def joined(x, m):
        left = ahead(strip(x, m), m // splits)
        right = ahead(strip(x, m + 1), (m + 1) // splits - LANES // 2)
        return jnp.where(low, left, right)

    for c in range(half):
        padded[:used, :] = lanes_ref[0, c].astype(jnp.float32)
        lanes = padded[...].T
        steps = taps // SHIFTS + 1
        for m in range(steps + 2):
            pair = joined(lanes, m).astype(jnp.bfloat16)
            if m < steps:
                hankel[c, m * SHIFTS : (m + 1) * SHIFTS, :LANES] = pair
            if m >= 2:
                hankel[c, (m - 2) * SHIFTS : (m - 1) * SHIFTS, LANES:] = pair
        squares = lanes * lanes
        high = squares.astype(jnp.bfloat16)
        rest = (squares - high.astype(jnp.float32)).astype(jnp.bfloat16)
        sums = jnp.dot(
            steps_ref[...],
            jnp.concatenate([high, rest], axis=1),
            preferred_element_type=jnp.float32,
        )
        sums = sums[:, :LANES] + sums[:, LANES:]
        before, suffix = sums[:LANES], sums[LANES:]
        total = suffix[0:1]
        middle = jnp.zeros_like(total)
        for by in range(1, whole):
            middle = middle + ahead(total, by)
        energy = suffix + middle + ahead(before, whole)
        root = lax.rsqrt(energy / taps + EPSILON)
        scale[c, :, :LANES] = joined(root, 0)
        scale[c, :, LANES:] = joined(root, 2)

    first, last = start_ref[block], start_ref[block + 1]

    def chunk(number, carry):
        base = first + number * GROUP
        for g in range(GROUP):
            pair = order_ref[base + g]
            rows = filters_ref[pair]
            for c in range(half):
                spread = jnp.broadcast_to(rows[c : c + 1], (SHIFTS, depth))
                spread = pltpu.roll(spread, 0, 1, stride=1, stride_axis=0)
                skewed[c, g * SHIFTS : (g + 1) * SHIFTS, :] = spread.astype(jnp.bfloat16)
        totals = [None] * GROUP
        for c in range(half):
            raw = jnp.dot(skewed[c], hankel[c], preferred_element_type=jnp.float32)
            for g in range(GROUP):
                pair = order_ref[base + g]
                term = raw[g * SHIFTS : (g + 1) * SHIFTS] * (scale[c] * gain_ref[pair * half + c])
                totals[g] = term if c == 0 else totals[g] + term
        for g in range(GROUP):
            place = jnp.where(base + g < last, lax.div(order_ref[base + g], 2), templates)
            totals_ref[place] += totals[g]
        return carry

    lax.fori_loop(0, lax.div(last - first + GROUP - 1, GROUP), chunk, 0)

    @pl.when(block == pl.num_programs(0) - 1)
    def _():
        rows = keep_ref.shape[2]

        batch = turned.shape[0]

        def turn(number, carry):
            for j in range(batch):
                k = number * batch + j
                left, right = totals_ref[k, :, :LANES], totals_ref[k, :, LANES:]
                stack = [left, ahead(left, LANES // 2), right, ahead(right, LANES // 2)]
                turned[j] = jnp.concatenate(stack, axis=0).T[: LANES // 2]
            for slot in range(parts):
                piece = lax.bitwise_xor(me_ref[0], slot)
                at = pl.ds(pl.multiple_of(piece * rows, 8), rows)
                target = send_ref if slot & 1 else keep_ref
                for j in range(batch):
                    target[slot >> 1, number * batch + j] = turned[j, at, :]
            return carry

        lax.fori_loop(0, templates // batch, turn, 0)


def correlate(arrived, filters, sources, axis):
    blocks, half, window = arrived.shape
    templates = filters.shape[0]
    taps = filters.shape[2]
    pairs = templates * 2
    lags = window - taps
    parts = lax.axis_size(axis)
    cols = lags // SHIFTS
    assert cols == 2 * LANES and LANES == 4 * SHIFTS
    used = window // LANES
    depth = -(-(taps + SHIFTS) // LANES) * LANES
    lanes = arrived.reshape(blocks, half, used, LANES)
    wide = filters.astype(jnp.float32)
    gain = 1.0 / (taps * jnp.sqrt(jnp.mean(wide * wide, axis=2) + EPSILON))
    padded = jnp.pad(wide.reshape(pairs, half, taps), ((0, 0), (0, 0), (0, depth - taps)))

    named = sources.reshape(pairs)
    ids = jnp.arange(pairs, dtype=jnp.int32)
    ahead = (named[None, :] < named[:, None]) | (
        (named[None, :] == named[:, None]) & (ids[None, :] < ids[:, None])
    )
    place = jnp.sum(ahead.astype(jnp.int32), axis=1)
    spots = jnp.arange(pairs + GROUP, dtype=jnp.int32)
    order = jnp.sum(jnp.where(place[None, :] == spots[:, None], ids[None, :], 0), axis=1)
    edges = jnp.arange(blocks + 1, dtype=jnp.int32)
    start = jnp.sum((named[None, :] < edges[:, None]).astype(jnp.int32), axis=1)

    spots = jnp.arange(LANES)
    earlier = spots[None, :] < spots[:, None]
    steps = jnp.concatenate([earlier, ~earlier], axis=0).astype(jnp.bfloat16)
    me = lax.axis_index(axis).astype(jnp.int32).reshape(1)
    dims = (templates, half, taps, used, depth, parts)
    smem = pl.BlockSpec(memory_space=pltpu.SMEM)
    piece = (parts // 2, templates, lags // LANES // parts, LANES)
    piece_spec = pl.BlockSpec(piece, lambda b: (0, 0, 0, 0))
    return pl.pallas_call(
        functools.partial(correlate_kernel, dims),
        grid=(blocks,),
        out_shape=[jax.ShapeDtypeStruct(piece, jnp.float32)] * 2,
        in_specs=[
            smem,
            smem,
            smem,
            smem,
            pl.BlockSpec((2 * LANES, LANES), lambda b: (0, 0)),
            pl.BlockSpec((1, half, used, LANES), lambda b: (b, 0, 0, 0)),
            pl.BlockSpec((pairs, half, depth), lambda b: (0, 0, 0)),
        ],
        out_specs=[piece_spec, piece_spec],
        scratch_shapes=[
            pltpu.VMEM((templates + 1, SHIFTS, cols), jnp.float32),
            pltpu.VMEM((LANES, LANES), jnp.float32),
            pltpu.VMEM((half, depth, cols), jnp.bfloat16),
            pltpu.VMEM((half, GROUP * SHIFTS, depth), jnp.bfloat16),
            pltpu.VMEM((half, SHIFTS, cols), jnp.float32),
            pltpu.VMEM((math.gcd(templates, 13), LANES // 2, LANES), jnp.float32),
        ],
        compiler_params=pltpu.CompilerParams(vmem_limit_bytes=40 * 1024 * 1024),
        name="correlate",
    )(me, start, order, gain.reshape(-1), steps, lanes, padded)


def swapped(x, axis, bit):
    return lax.ppermute(x, axis, [(i, i ^ bit) for i in range(lax.axis_size(axis))])


def per_device(waveform, templates, block_of, trace_of):
    own_index = lax.axis_index("st")
    station_count = lax.axis_size("st")
    own_templates = templates.shape[0]
    group_chans = templates.shape[1]
    half_chans = group_chans // 2
    window = waveform.shape[2]
    sources = block_of[0].reshape(station_count, own_templates, 2)
    own_sources = lax.dynamic_index_in_dim(sources, own_index, 0, keepdims=False)
    wanted = lax.dynamic_index_in_dim(trace_of[0], own_index, 1, keepdims=False)
    wanted = wanted.reshape(-1)
    station = (wanted * 43691) >> 17
    source_rows = waveform[station, wanted - 3 * station]
    arrived = lax.all_to_all(
        source_rows.reshape(station_count, half_chans, window),
        "st",
        split_axis=0,
        concat_axis=0,
        tiled=True,
    )
    keep, send = correlate(arrived, templates, own_sources, "ch")
    bit = 1
    while True:
        keep = keep + swapped(send, "ch", bit)
        if keep.shape[0] == 1:
            break
        halves = keep.reshape(keep.shape[0] // 2, 2, *keep.shape[1:])
        keep, send = halves[:, 0], halves[:, 1]
        bit *= 2
    return keep.reshape(own_templates, -1)


def solution(mesh):
    in_specs = (
        P("st", None, None),
        P("st", "ch", None),
        P("ch", None, None),
        P("ch", None, None, None),
    )
    out_specs = P("st", "ch")
    return jax.shard_map(
        per_device, mesh=mesh, in_specs=in_specs, out_specs=out_specs, check_vma=False
    )
```
